128 devices in a mesh: ij: 2 (over x_lo), ab: 16 (over y, x_hi, core), cd: 4 (over z).
Axes of the slice: x: 4 (x_hi: 2, x_lo: 2; x = x_hi * 2 + x_lo), y: 4, z: 4, core: 2. Of those that a mesh axis runs over, the one named last changes fastest.
Arguments:
- amplitudes: float32 [2048, 16384], P('ab', ('ij', 'cd')), may hold values from -6 to 6
- integrals: float32 [16384, 16384], P('ab', ('ij', 'cd')), may hold values from -0.046875 to 0.046875
- occupied_label: int32 [16], replicated, may hold values from 0 to 3
- outer_label: int32 [128], replicated, may hold values from 0 to 3
- inner_label: int32 [128], replicated, may hold values from 0 to 3
Outputs:
- ladder_term: float32 [2048, 16384], P(('ij', 'cd'), 'ab')
The draws below stay inside these ranges and needn't reach their ends.
Inputs may be any that keep to these rules, and one draw needn't show every extreme that they name: `occupied_label`: each label names the symmetry block of one tile; tiles couple only where labels agree. `outer_label`: labels of the outer tiles, as above. `inner_label`: labels of the contracted tiles, as above.
All inputs are finite; a program needn't handle non-finite values.
Results may differ from the reference program's by a relative error of at most 0.000073.
Values sent between devices are 32-bit elements; how exact they have to be, the bound alone decides.
No kernel may reach another device: no remote copies, remote signals or barrier semaphores. Data moves between devices by JAX's collectives and lax.ppermute only.
A program may use at most 192 MiB of HBM per device.

```python
import math
import jax
import jax.numpy as jnp
import numpy as np
from jax import lax

TILE = 128
AB = 16384
CD = 16384
IJ = 2048


def plant(drawn, key, low, high):
    longest = drawn.shape.index(max(drawn.shape))
    spots = []
    for shift in (0, 1):
        where = [jax.random.randint(jax.random.fold_in(key, axis), (), 0, length) for axis, length in enumerate(drawn.shape)]
        where[longest] = (where[longest] + shift) % drawn.shape[longest]
        spots.append(tuple(where))
    return drawn.at[spots[0]].set(low).at[spots[1]].set(high)


def with_spikes(drawn, key, source, target, shards_of, factor):
    def block_of(position):
        return (jnp.arange(drawn.shape[position]) // (drawn.shape[position] // shards_of)).reshape((-1,) + (1,) * (drawn.ndim - 1 - position))

    near = jax.random.permutation(key, shards_of)[block_of(target)]
    second = (block_of(target) + shards_of // 2) % shards_of
    return jnp.where((block_of(source) == near) | (block_of(source) == second), factor * drawn, drawn)


def shard_levels(own_key, shape, cuts, low, high):
    loudness = 1.0
    for dim, blocks in cuts:
        heights = jax.random.uniform(jax.random.fold_in(jax.random.fold_in(own_key, 6), dim), (blocks,), jnp.float32, low / len(cuts), high / len(cuts))
        loudness = loudness * jnp.repeat(jnp.exp(heights), shape[dim] // blocks).reshape((-1,) + (1,) * (len(shape) - 1 - dim))
    return loudness


def rank_bounds(amount, skew):
    portions = [(1 << 20) // math.isqrt(rank ** skew) + 1 for rank in range(1, amount + 1)]
    scale = 1 + sum(portions) // (1 << 30)
    return np.cumsum(np.array([max(1, weight // scale) for weight in portions]))


def ranked(rng, shape, amount, slope):
    table = rank_bounds(amount, slope)
    pick = jax.random.randint(jax.random.fold_in(rng, 1), shape, 0, int(table[amount - 1]))
    grade = jnp.searchsorted(jnp.asarray(table, jnp.int32), pick, side="right")
    return jax.random.permutation(jax.random.fold_in(rng, 2), amount)[grade].astype(jnp.int32)


def scatter_about(rng, dims, scale, bound, split=(), kind=jnp.bfloat16):
    level = shard_levels(rng, dims, split, -0.22, 0.18) if split else 1.0
    drawn = jax.random.normal(rng, dims, jnp.float32) * scale * level
    return jnp.minimum(jnp.maximum(drawn, -bound), bound).astype(kind)


def heavy_noise(own_key, extent, width, bound, shards, heavy, kind=jnp.bfloat16):
    entries = width * jax.random.normal(own_key, extent, jnp.float32)
    if shards:
        entries = entries * shard_levels(own_key, extent, shards, -0.22, 0.18)
    return jnp.clip(with_spikes(entries, jax.random.fold_in(own_key, 3), *heavy), -bound, bound).astype(kind)


def setup_inputs(seed: int = 0) -> dict:
    seeds = jax.random.split(jax.random.key(seed), 6)
    return {
        "amplitudes": heavy_noise(seeds[0], (IJ, CD), 1.0, 6.0, ((0, 16), (1, 8)), (1, 0, 16, 2.0), jnp.float32),
        "integrals": scatter_about(seeds[1], (AB, CD), CD ** -0.5, 0.046875, ((0, 16), (1, 8)), jnp.float32),
        "occupied_label": plant(ranked(seeds[2], (IJ // TILE,), 4, 3), jax.random.fold_in(seeds[2], 3), 0, 3).astype(jnp.int32),
        "outer_label": plant(ranked(seeds[3], (AB // TILE,), 4, 3), jax.random.fold_in(seeds[3], 3), 0, 3).astype(jnp.int32),
        "inner_label": plant(ranked(seeds[4], (CD // TILE,), 4, 3), jax.random.fold_in(seeds[4], 3), 0, 3).astype(jnp.int32),
    }


def reference(amplitudes, integrals, occupied_label, outer_label, inner_label):
    occupied_rows = jnp.repeat(occupied_label, TILE)
    outer_rows = jnp.repeat(outer_label, TILE)
    inner_cols = jnp.repeat(inner_label, TILE)
    amp_masked = jnp.where(occupied_rows[:, None] == inner_cols[None, :], amplitudes, jnp.zeros((), amplitudes.dtype))
    int_masked = jnp.where(outer_rows[:, None] == inner_cols[None, :], integrals, jnp.zeros((), integrals.dtype))
    return lax.dot_general(amp_masked, int_masked, (((1,), (1,)), ((), ())), precision=lax.Precision.HIGHEST, preferred_element_type=jnp.float32)
```

```python
import functools

import jax
import jax.numpy as jnp
from jax import lax
from jax.experimental import pallas as pl
from jax.experimental.pallas import tpu as pltpu
from jax.sharding import PartitionSpec as P

TILE = 128
LABELS = 4
CAPS_T = (8, 12, 16)
CAPS_R = ((12, 8), (16, 13), (22, 14), (32, 16))
ROWS = 16
COLS = 16
OUTS = 8
SMEM = pl.BlockSpec(memory_space=pltpu.SMEM)
HBM = pl.BlockSpec(memory_space=pl.ANY)
VMEM = pl.BlockSpec(memory_space=pltpu.VMEM)


def ab_index(y, xh, k):
    return y * 4 + xh * 2 + k


PLACES = [(y, xh, k) for y in range(4) for xh in range(2) for k in range(2)]
CORE_SWAP = [(ab_index(y, x, k), ab_index(y, x, 1 - k)) for y, x, k in PLACES]
X_SWAP = [(ab_index(y, x, k), ab_index(y, 1 - x, k)) for y, x, k in PLACES]
Y_UP = [(ab_index(y, x, k), ab_index((y + 1) % 4, x, k)) for y, x, k in PLACES]
Y_DOWN = [(ab_index(y, x, k), ab_index((y + 3) % 4, x, k)) for y, x, k in PLACES]
Z_UP = [(c, (c + 1) % 4) for c in range(4)]
Z_DOWN = [(c, (c + 3) % 4) for c in range(4)]


def where_am_i():
    block = lax.axis_index("ij") * 4 + lax.axis_index("cd")
    device_row = lax.axis_index("ab")
    return block, device_row, device_row // 4, (device_row // 2) % 2, device_row % 2


def count_labels(labels, first, size, counts, base):
    for label in range(LABELS):
        counts[base + label] = 0

    def add(at, carry):
        counts[base + labels[first + at]] += 1
        return carry

    lax.fori_loop(0, size, add, 0)


def plan_kernel(occ, outer, inner, amp_pick, out_pick, first_rows, counts):
    def amp_block(block, need):
        count_labels(inner, block * COLS, COLS, counts, 0)

        def chip_need(chip, need):
            return jnp.maximum(need, counts[occ[2 * chip]] + counts[occ[2 * chip + 1]])

        return lax.fori_loop(0, ROWS // 2, chip_need, need)

    need = lax.fori_loop(0, 8, amp_block, jnp.int32(0))
    pick = jnp.int32(0)
    for cap in CAPS_T[:-1]:
        pick += (need > 2 * cap).astype(jnp.int32)
    amp_pick[0] = pick

    def out_block(block, needs):
        count_labels(outer, block * OUTS, OUTS, counts, 0)

        def dest(c, needs):
            need_w, need_z = needs
            low = counts[occ[2 * c]] + counts[occ[2 * c + 1]]
            high = counts[occ[2 * c + 8]] + counts[occ[2 * c + 9]]
            return jnp.maximum(need_w, jnp.maximum(low, high)), jnp.maximum(need_z, low + high)

        return lax.fori_loop(0, 4, dest, needs)

    need_w, need_z = lax.fori_loop(0, ROWS, out_block, (jnp.int32(0), jnp.int32(0)))
    pick = jnp.int32(0)
    for cap_z, cap_w in CAPS_R[:-1]:
        pick += jnp.logical_or(need_w > cap_w, need_z > cap_z).astype(jnp.int32)
    out_pick[0] = pick
    count_labels(outer, lax.axis_index("ab") * OUTS, OUTS, counts, 0)
    c = lax.axis_index("cd")
    first_rows[0] = counts[occ[2 * c]] + counts[occ[2 * c + 1]]


def plan(occ, outer, inner):
    one = jax.ShapeDtypeStruct((1,), jnp.int32)
    return pl.pallas_call(
        plan_kernel,
        out_shape=(one, one, one),
        in_specs=[SMEM] * 3,
        out_specs=(SMEM, SMEM, SMEM),
        scratch_shapes=[pltpu.SMEM((LABELS,), jnp.int32)],
        name="plan_capacities",
    )(occ, outer, inner)


def pack_kernel(occ, inner, mine, other, packed, sem):
    block, _, y, xh, k = where_am_i()
    chip = y * 2 + xh

    def tile(ref, c):
        return ref.at[:, pl.ds(pl.multiple_of(c * TILE, TILE), TILE)]

    def issue(core, first):
        label = occ[chip * 2 + core]

        def one(c, p):
            hit = inner[block * COLS + c] == label

            @pl.when(jnp.logical_and(hit, core == k))
            def _():
                pltpu.make_async_copy(tile(mine, c), packed.at[p], sem.at[p]).start()

            @pl.when(jnp.logical_and(hit, core != k))
            def _():
                pltpu.make_async_copy(tile(other, c), packed.at[p], sem.at[p]).start()

            return p + hit.astype(jnp.int32)

        return lax.fori_loop(0, COLS, one, first)

    count = issue(1, issue(0, jnp.int32(0)))

    def drain(p, carry):
        pltpu.make_async_copy(tile(mine, 0), packed.at[p], sem.at[p]).wait()
        return carry

    lax.fori_loop(0, count, drain, 0)


def pack(occ, inner, mine, other):
    return pl.pallas_call(
        pack_kernel,
        out_shape=jax.ShapeDtypeStruct((2 * COLS, TILE, TILE), jnp.float32),
        in_specs=[SMEM, SMEM, HBM, HBM],
        out_specs=HBM,
        scratch_shapes=[pltpu.SemaphoreType.DMA((2 * COLS,))],
        name="pack_amplitudes",
    )(occ, inner, mine, other)


def split(x):
    hi = x.astype(jnp.bfloat16)
    lo = (x - hi.astype(jnp.float32)).astype(jnp.bfloat16)
    return hi, lo


def split_kernel(outer, inner, ints, hi, lo, buf, sem):
    block, device_row, _, _, _ = where_am_i()
    col0 = block * COLS
    out0 = device_row * OUTS

    def copy(t, c, p):
        return pltpu.make_async_copy(
            ints.at[pl.ds(pl.multiple_of(t * TILE, TILE), TILE), pl.ds(pl.multiple_of(c * TILE, TILE), TILE)],
            buf.at[t * COLS + p],
            sem.at[t * COLS + p],
        )

    def count(t, use):
        label = outer[out0 + t]

        def one(c, p):
            hit = inner[col0 + c] == label
            if use:

                @pl.when(hit)
                def _():
                    copy(t, c, p).start()

            return p + hit.astype(jnp.int32)

        return lax.fori_loop(0, COLS, one, jnp.int32(0))

    def issue(t, carry):
        count(t, True)
        return carry

    lax.fori_loop(0, OUTS, issue, 0)

    def split_all(t, carry):
        def one(p, inner_carry):
            copy(t, 0, p).wait()
            at = t * COLS + p
            hi[at], lo[at] = split(buf[at])
            return inner_carry

        return lax.fori_loop(0, count(t, False), one, carry)

    lax.fori_loop(0, OUTS, split_all, 0)


def split_integrals(outer, inner, ints):
    part = jax.ShapeDtypeStruct((OUTS * COLS, TILE, TILE), jnp.bfloat16)
    return pl.pallas_call(
        split_kernel,
        out_shape=(part, part),
        in_specs=[SMEM, SMEM, HBM],
        out_specs=(VMEM, VMEM),
        scratch_shapes=[
            pltpu.VMEM((OUTS * COLS, TILE, TILE), jnp.float32),
            pltpu.SemaphoreType.DMA((OUTS * COLS,)),
        ],
        compiler_params=pltpu.CompilerParams(vmem_limit_bytes=20 * 1024 * 1024),
        cost_estimate=pl.CostEstimate(flops=1 << 24, bytes_accessed=16 << 20, transcendentals=0),
        name="split_integrals",
    )(outer, inner, ints)


def pieces(cap):
    half = cap // 2
    rest = cap - half
    same = [
        (1, 0, cap, 0, 0, 1, 0),
        (2, 0, cap, 0, 3, 0, 0),
        (3, 0, cap, 0, 1, 0, 0),
        (4, 0, cap, 0, 3, 1, 0),
        (4, cap, half, 0, 2, 0, 0),
        (5, 0, cap, 0, 1, 1, 0),
        (5, cap, rest, 0, 2, 0, half),
        (6, 0, half, 0, 2, 1, 0),
        (7, 0, rest, 0, 2, 1, half),
    ]
    start = {1: (8, 0), 2: (8, cap), 3: (8, 2 * cap), 4: (9, 0), 5: (9, cap + half), 6: (10, 0), 7: (10, half)}
    swapped = [
        (start[at][0], start[at][1] + offset, size, 1, dy, dx, first)
        for at, offset, size, _, dy, dx, first in same
    ]
    return same + swapped


def ladder_kernel(cap, occ, outer, inner, ints_hi, ints_lo, *refs):
    lists = refs[:11]
    part, amp_buf, int_hi, int_lo, out_buf, row_n, row_at, out_n, out_at, in_n, amp_sem, int_sem, out_sem = refs[11:]
    block, device_row, y, xh, k = where_am_i()
    col0 = block * COLS
    out0 = device_row * OUTS

    int_copies = [
        pltpu.make_async_copy(ints_hi, int_hi, int_sem.at[0]),
        pltpu.make_async_copy(ints_lo, int_lo, int_sem.at[1]),
    ]
    for copy in int_copies:
        copy.start()
    count_labels(inner, col0, COLS, in_n, 0)

    def fill_amps(src, offset, size, chip, first):
        used = in_n[occ[2 * chip]] + in_n[occ[2 * chip + 1]]

        def one(q, carry):
            at = chip * 2 * cap + first + q
            pltpu.make_async_copy(src.at[offset + q], amp_buf.at[at], amp_sem.at[at]).start()
            return carry

        lax.fori_loop(0, jnp.clip(used - first, 0, size), one, 0)

    fill_amps(lists[0], 0, 2 * cap, y * 2 + xh, 0)
    for at, offset, size, swapped, dy, dx, first in pieces(cap):
        core = k ^ swapped
        fill_amps(lists[at], offset, size, ((y + dy) % 4) * 2 + (xh + dx) % 2, core * cap + first)

    for label in range(LABELS):
        row_n[label] = 0
        out_n[label] = 0

    def list_rows(r, carry):
        label = occ[r]
        row_at[label * ROWS + row_n[label]] = r
        row_n[label] += 1
        return carry

    lax.fori_loop(0, ROWS, list_rows, 0)

    def list_outs(t, carry):
        label = outer[out0 + t]
        out_at[label * OUTS + out_n[label]] = t
        out_n[label] += 1
        return carry

    lax.fori_loop(0, OUTS, list_outs, 0)

    def wait_amps(chip, carry):
        def one(p, inner_carry):
            at = chip * 2 * cap + p
            pltpu.make_async_copy(lists[0].at[0], amp_buf.at[at], amp_sem.at[at]).wait()
            return inner_carry

        return lax.fori_loop(0, in_n[occ[2 * chip]] + in_n[occ[2 * chip + 1]], one, carry)

    lax.fori_loop(0, ROWS // 2, wait_amps, 0)
    for copy in int_copies:
        copy.wait()

    def out_copy(dest, slot):
        return pltpu.make_async_copy(
            out_buf.at[dest * 4 * OUTS + slot], part.at[dest, slot], out_sem.at[dest * 4 * OUTS + slot]
        )

    def per_label(label, carry):
        n_rows, n_outs, n_in = row_n[label], out_n[label], in_n[label]

        def block_of(buf, at0, at1, p, width):
            return jnp.concatenate(
                [jnp.concatenate([buf[at + p + w] for w in range(width)], axis=1) for at in (at0, at1)], axis=0
            )

        def per_rows(rp, carry):
            m0 = 2 * rp
            m1 = jnp.minimum(m0 + 1, n_rows - 1)
            r0, r1 = row_at[label * ROWS + m0], row_at[label * ROWS + m1]

            def list_start(r):
                chip = r // 2
                return chip * 2 * cap + jnp.where(r % 2 == 1, in_n[occ[2 * chip]], 0)

            a0, a1 = list_start(r0), list_start(r1)

            def per_outs(up, carry):
                q0 = 2 * up
                q1 = jnp.minimum(q0 + 1, n_outs - 1)
                b0, b1 = out_at[label * OUTS + q0] * COLS, out_at[label * OUTS + q1] * COLS

                def step(width, first):
                    def run(pp, total):
                        p = first + pp * width
                        left_hi, left_lo = split(block_of(amp_buf, a0, a1, p, width))
                        right_hi, right_lo = block_of(int_hi, b0, b1, p, width), block_of(int_lo, b0, b1, p, width)

                        def dot(a, b):
                            return lax.dot_general(
                                a, b, (((1,), (1,)), ((), ())), preferred_element_type=jnp.float32
                            )

                        return total + (dot(left_lo, right_hi) + dot(left_hi, right_lo) + dot(left_hi, right_hi))

                    return run

                total = jnp.zeros((2 * TILE, 2 * TILE), jnp.float32)
                total = lax.fori_loop(0, n_in // 2, step(2, 0), total)
                total = lax.fori_loop(0, n_in % 2, step(1, n_in // 2 * 2), total)
                for rr in range(2):
                    r = (r0, r1)[rr]
                    dest = (r // 2) % 4
                    before = jnp.where(r % 2 == 1, out_n[occ[r // 2 * 2]], 0)
                    low = out_n[occ[dest * 2]] + out_n[occ[dest * 2 + 1]]
                    before += jnp.where(r >= 8, low, 0)
                    for tt in range(2):
                        fresh = jnp.bool_(True)
                        if rr:
                            fresh = jnp.logical_and(fresh, m1 > m0)
                        if tt:
                            fresh = jnp.logical_and(fresh, q1 > q0)
                        value = total[rr * TILE : (rr + 1) * TILE, tt * TILE : (tt + 1) * TILE]

                        @pl.when(fresh)
                        def _(dest=dest, slot=before + (q0, q1)[tt], value=value):
                            out_buf[dest * 4 * OUTS + slot] = value
                            out_copy(dest, slot).start()

                return carry

            return lax.fori_loop(0, (n_outs + 1) // 2, per_outs, carry)

        return lax.fori_loop(0, (n_rows + 1) // 2, per_rows, carry)

    lax.fori_loop(0, LABELS, per_label, 0)

    def drain_outs(dest, carry):
        def drain(slot, inner_carry):
            out_copy(dest, slot).wait()
            return inner_carry

        count = jnp.int32(0)
        for r in (0, 1, 8, 9):
            count += out_n[occ[dest * 2 + r]]
        return lax.fori_loop(0, count, drain, carry)

    lax.fori_loop(0, 4, drain_outs, 0)


def ladder(cap, occ, outer, inner, ints_hi, ints_lo, lists):
    amps = ROWS * cap
    return pl.pallas_call(
        functools.partial(ladder_kernel, cap),
        out_shape=jax.ShapeDtypeStruct((4, 4 * OUTS, TILE, TILE), jnp.float32),
        in_specs=[SMEM] * 3 + [HBM] * (2 + len(lists)),
        out_specs=HBM,
        scratch_shapes=[
            pltpu.VMEM((amps, TILE, TILE), jnp.float32),
            pltpu.VMEM((OUTS * COLS, TILE, TILE), jnp.bfloat16),
            pltpu.VMEM((OUTS * COLS, TILE, TILE), jnp.bfloat16),
            pltpu.VMEM((OUTS * COLS, TILE, TILE), jnp.float32),
            pltpu.SMEM((LABELS,), jnp.int32),
            pltpu.SMEM((LABELS * ROWS,), jnp.int32),
            pltpu.SMEM((LABELS,), jnp.int32),
            pltpu.SMEM((LABELS * OUTS,), jnp.int32),
            pltpu.SMEM((LABELS,), jnp.int32),
            pltpu.SemaphoreType.DMA((amps,)),
            pltpu.SemaphoreType.DMA((2,)),
            pltpu.SemaphoreType.DMA((OUTS * COLS,)),
        ],
        compiler_params=pltpu.CompilerParams(vmem_limit_bytes=(18 + cap) * 1024 * 1024),
        name="ladder_tiles",
    )(occ, outer, inner, ints_hi, ints_lo, *lists)


def gather_and_multiply(cap, packed, occ, outer, inner, ints):
    half = cap // 2
    core = lax.axis_index("ab") % 2
    send = functools.partial(lax.ppermute, axis_name="ab")
    own = lax.dynamic_slice_in_dim(packed, core * cap, cap)
    x_own = send(own, perm=X_SWAP)
    up = send(own, perm=Y_UP)
    down = send(own, perm=Y_DOWN)
    up_two = send(jnp.concatenate([x_own, up[:half]]), perm=Y_UP)
    down_two = send(jnp.concatenate([x_own, down[half:]]), perm=Y_DOWN)
    ints_hi, ints_lo = split_integrals(outer, inner, ints)
    up_two, down_two, ints_hi, ints_lo = lax.optimization_barrier((up_two, down_two, ints_hi, ints_lo))
    up_three = send(up_two[:half], perm=Y_UP)
    down_three = send(down_two[half:cap], perm=Y_DOWN)
    lists = [packed, x_own, up, down, up_two, down_two, up_three, down_three]
    lists.append(send(jnp.concatenate([x_own, up, down]), perm=CORE_SWAP))
    lists.append(send(jnp.concatenate([up_two, down_two]), perm=CORE_SWAP))
    lists.append(send(jnp.concatenate([up_three, down_three]), perm=CORE_SWAP))
    return ladder(cap, occ, outer, inner, ints_hi, ints_lo, lists)


def place_kernel(cap_z, cap_w, occ, outer, first_rows, mine, other, out):
    block, device_row, _, _, _ = where_am_i()
    skip = jnp.maximum(first_rows[0] - (cap_z - cap_w), 0)
    slot = jnp.where(block >= 4, skip, 0)
    for r in range(2):
        label = occ[block * 2 + r]
        for t in range(OUTS):
            hit = outer[device_row * OUTS + t] == label
            at = jnp.minimum(slot, cap_w - 1)
            value = mine[at] + other[at]
            out[r * TILE : (r + 1) * TILE, t * TILE : (t + 1) * TILE] = jnp.where(
                hit, value, jnp.zeros_like(value)
            )
            slot = slot + hit.astype(jnp.int32)


def place(cap_z, cap_w, occ, outer, first_rows, mine, other):
    return pl.pallas_call(
        functools.partial(place_kernel, cap_z, cap_w),
        out_shape=jax.ShapeDtypeStruct((2 * TILE, OUTS * TILE), jnp.float32),
        in_specs=[SMEM] * 3 + [VMEM] * 2,
        out_specs=VMEM,
        compiler_params=pltpu.CompilerParams(vmem_limit_bytes=16 * 1024 * 1024),
        name="place_tiles",
    )(occ, outer, first_rows, mine, other)


def reduce_and_place(caps, part, occ, outer, first_rows):
    cap_z, cap_w = caps
    half = cap_z // 2
    c = lax.axis_index("cd")
    i = lax.axis_index("ij")
    send = functools.partial(lax.ppermute, axis_name="cd")

    def tiles(shift, first, size):
        return lax.dynamic_slice(part, ((c + shift) % 4, first, 0, 0), (1, size, TILE, TILE))[0]

    rest = cap_z - half
    up_far = send(tiles(2, 0, half), perm=Z_UP)
    down_far = send(tiles(2, half, rest), perm=Z_DOWN)
    from_down = send(jnp.concatenate([tiles(1, 0, half) + up_far, tiles(1, half, rest)]), perm=Z_UP)
    from_up = send(jnp.concatenate([tiles(3, 0, half), tiles(3, half, rest) + down_far]), perm=Z_DOWN)
    total = tiles(0, 0, cap_z) + from_down + from_up
    high = jnp.minimum(first_rows[0], cap_z - cap_w)
    mine = lax.dynamic_slice_in_dim(total, jnp.where(i == 1, high, 0), cap_w)
    theirs = lax.dynamic_slice_in_dim(total, jnp.where(i == 1, 0, high), cap_w)
    other = lax.ppermute(theirs, "ij", [(0, 1), (1, 0)])
    return place(cap_z, cap_w, occ, outer, first_rows, mine, other)


def shards(amplitudes, integrals, occupied_label, outer_label, inner_label):
    others = lax.ppermute(amplitudes, "ab", CORE_SWAP)
    amp_pick, out_pick, first_rows = plan(occupied_label, outer_label, inner_label)
    packed = pack(occupied_label, inner_label, amplitudes, others)
    part = lax.switch(
        amp_pick[0],
        [functools.partial(gather_and_multiply, cap) for cap in CAPS_T],
        packed, occupied_label, outer_label, inner_label, integrals,
    )
    return lax.switch(
        out_pick[0],
        [functools.partial(reduce_and_place, caps) for caps in CAPS_R],
        part, occupied_label, outer_label, first_rows,
    )


def solution(mesh):
    placed = (P("ab", ("ij", "cd")), P("ab", ("ij", "cd")), P(), P(), P())
    return jax.shard_map(
        shards, mesh=mesh, in_specs=placed, out_specs=P(("ij", "cd"), "ab"), check_vma=False
    )
```

```python
import functools

import jax
import jax.numpy as jnp
from jax import lax
from jax.experimental import pallas as pl
from jax.experimental.pallas import tpu as pltpu
from jax.sharding import PartitionSpec as P

TILE = 128
LABELS = 4
CAPS_T = (8, 12, 16)
CAPS_R = ((13, 9), (22, 14), (32, 16))
ROW_BLOCK = 4
OUT_BLOCK = 2
ROWS = 16
COLS = 16
OUTS = 8
SMEM = pl.BlockSpec(memory_space=pltpu.SMEM)
HBM = pl.BlockSpec(memory_space=pl.ANY)
VMEM = pl.BlockSpec(memory_space=pltpu.VMEM)


def ab_index(y, xh, k):
    return y * 4 + xh * 2 + k


PLACES = [(y, xh, k) for y in range(4) for xh in range(2) for k in range(2)]
CORE_SWAP = [(ab_index(y, x, k), ab_index(y, x, 1 - k)) for y, x, k in PLACES]
X_SWAP = [(ab_index(y, x, k), ab_index(y, 1 - x, k)) for y, x, k in PLACES]
Y_UP = [(ab_index(y, x, k), ab_index((y + 1) % 4, x, k)) for y, x, k in PLACES]
Y_DOWN = [(ab_index(y, x, k), ab_index((y + 3) % 4, x, k)) for y, x, k in PLACES]
Z_UP = [(c, (c + 1) % 4) for c in range(4)]
Z_DOWN = [(c, (c + 3) % 4) for c in range(4)]


def where_am_i():
    block = lax.axis_index("ij") * 4 + lax.axis_index("cd")
    device_row = lax.axis_index("ab")
    return block, device_row, device_row // 4, (device_row // 2) % 2, device_row % 2


def count_labels(labels, first, size, counts, base):
    for label in range(LABELS):
        counts[base + label] = 0

    def add(at, carry):
        counts[base + labels[first + at]] += 1
        return carry

    lax.fori_loop(0, size, add, 0)


def plan_kernel(occ, outer, inner, amp_pick, out_pick, first_rows, counts):
    def amp_block(block, need):
        count_labels(inner, block * COLS, COLS, counts, 0)

        def chip_need(chip, need):
            return jnp.maximum(need, counts[occ[2 * chip]] + counts[occ[2 * chip + 1]])

        return lax.fori_loop(0, ROWS // 2, chip_need, need)

    need = lax.fori_loop(0, 8, amp_block, jnp.int32(0))
    pick = jnp.int32(0)
    for cap in CAPS_T[:-1]:
        pick += (need > 2 * cap).astype(jnp.int32)
    amp_pick[0] = pick

    def out_block(block, needs):
        count_labels(outer, block * OUTS, OUTS, counts, 0)

        def dest(c, needs):
            need_w, need_z = needs
            low = counts[occ[2 * c]] + counts[occ[2 * c + 1]]
            high = counts[occ[2 * c + 8]] + counts[occ[2 * c + 9]]
            return jnp.maximum(need_w, jnp.maximum(low, high)), jnp.maximum(need_z, low + high)

        return lax.fori_loop(0, 4, dest, needs)

    need_w, need_z = lax.fori_loop(0, ROWS, out_block, (jnp.int32(0), jnp.int32(0)))
    pick = jnp.int32(0)
    for cap_z, cap_w in CAPS_R[:-1]:
        pick += jnp.logical_or(need_w > cap_w, need_z > cap_z).astype(jnp.int32)
    out_pick[0] = pick
    count_labels(outer, lax.axis_index("ab") * OUTS, OUTS, counts, 0)
    c = lax.axis_index("cd")
    first_rows[0] = counts[occ[2 * c]] + counts[occ[2 * c + 1]]


def plan(occ, outer, inner):
    one = jax.ShapeDtypeStruct((1,), jnp.int32)
    return pl.pallas_call(
        plan_kernel,
        out_shape=(one, one, one),
        in_specs=[SMEM] * 3,
        out_specs=(SMEM, SMEM, SMEM),
        scratch_shapes=[pltpu.SMEM((LABELS,), jnp.int32)],
        name="plan_capacities",
    )(occ, outer, inner)


def pack_kernel(occ, inner, mine, other, packed, sem):
    block, _, y, xh, k = where_am_i()
    chip = y * 2 + xh

    def tile(ref, c):
        return ref.at[:, pl.ds(pl.multiple_of(c * TILE, TILE), TILE)]

    def issue(core, first):
        label = occ[chip * 2 + core]

        def one(c, p):
            hit = inner[block * COLS + c] == label

            @pl.when(jnp.logical_and(hit, core == k))
            def _():
                pltpu.make_async_copy(tile(mine, c), packed.at[p], sem.at[p]).start()

            @pl.when(jnp.logical_and(hit, core != k))
            def _():
                pltpu.make_async_copy(tile(other, c), packed.at[p], sem.at[p]).start()

            return p + hit.astype(jnp.int32)

        return lax.fori_loop(0, COLS, one, first)

    count = issue(1, issue(0, jnp.int32(0)))

    def drain(p, carry):
        pltpu.make_async_copy(tile(mine, 0), packed.at[p], sem.at[p]).wait()
        return carry

    lax.fori_loop(0, count, drain, 0)


def pack(occ, inner, mine, other):
    return pl.pallas_call(
        pack_kernel,
        out_shape=jax.ShapeDtypeStruct((2 * COLS, TILE, TILE), jnp.float32),
        in_specs=[SMEM, SMEM, HBM, HBM],
        out_specs=HBM,
        scratch_shapes=[pltpu.SemaphoreType.DMA((2 * COLS,))],
        name="pack_amplitudes",
    )(occ, inner, mine, other)


def split(x):
    hi = x.astype(jnp.bfloat16)
    lo = (x - hi.astype(jnp.float32)).astype(jnp.bfloat16)
    return hi, lo


def split_kernel(outer, inner, ints, parts, buf, sem):
    block, device_row, _, _, _ = where_am_i()
    col0 = block * COLS
    out0 = device_row * OUTS

    def copy(t, c, p):
        return pltpu.make_async_copy(
            ints.at[pl.ds(pl.multiple_of(t * TILE, TILE), TILE), pl.ds(pl.multiple_of(c * TILE, TILE), TILE)],
            buf.at[t * COLS + p],
            sem.at[t * COLS + p],
        )

    def count(t, use):
        label = outer[out0 + t]

        def one(c, p):
            hit = inner[col0 + c] == label
            if use:

                @pl.when(hit)
                def _():
                    copy(t, c, p).start()

            return p + hit.astype(jnp.int32)

        return lax.fori_loop(0, COLS, one, jnp.int32(0))

    def issue(t, carry):
        count(t, True)
        return carry

    lax.fori_loop(0, OUTS, issue, 0)

    def split_all(t, carry):
        def one(p, inner_carry):
            copy(t, 0, p).wait()
            at = t * COLS + p
            parts[at, 0], parts[at, 1] = split(buf[at].T)
            return inner_carry

        return lax.fori_loop(0, count(t, False), one, carry)

    lax.fori_loop(0, OUTS, split_all, 0)


def split_integrals(outer, inner, ints):
    return pl.pallas_call(
        split_kernel,
        out_shape=jax.ShapeDtypeStruct((OUTS * COLS, 2, TILE, TILE), jnp.bfloat16),
        in_specs=[SMEM, SMEM, HBM],
        out_specs=VMEM,
        scratch_shapes=[
            pltpu.VMEM((OUTS * COLS, TILE, TILE), jnp.float32),
            pltpu.SemaphoreType.DMA((OUTS * COLS,)),
        ],
        compiler_params=pltpu.CompilerParams(vmem_limit_bytes=20 * 1024 * 1024),
        cost_estimate=pl.CostEstimate(flops=1 << 24, bytes_accessed=16 << 20, transcendentals=0),
        name="split_integrals",
    )(outer, inner, ints)


def pieces(cap):
    half = cap // 2
    rest = cap - half
    same = [
        (1, 0, cap, 0, 0, 1, 0),
        (2, 0, cap, 0, 3, 0, 0),
        (3, 0, cap, 0, 1, 0, 0),
        (4, 0, half, 0, 3, 1, 0),
        (4, half, half, 0, 2, 0, 0),
        (5, 0, rest, 0, 1, 1, half),
        (5, rest, rest, 0, 2, 0, half),
        (6, 0, rest, 0, 3, 1, half),
        (6, rest, half, 0, 1, 1, 0),
        (7, 0, half, 0, 2, 1, 0),
        (8, 0, rest, 0, 2, 1, half),
    ]
    start = {
        1: (9, 0), 2: (9, cap), 3: (9, 2 * cap),
        4: (9, 3 * cap), 5: (9, 3 * cap + 2 * half), 6: (9, 5 * cap),
        7: (10, 0), 8: (10, half),
    }
    swapped = [
        (start[at][0], start[at][1] + offset, size, 1, dy, dx, first)
        for at, offset, size, _, dy, dx, first in same
    ]
    return same + swapped


def ladder_kernel(cap, occ, outer, inner, ints, *refs):
    lists = refs[:11]
    part, amp_buf, int_buf, out_buf, row_n, row_at, out_n, out_at, in_n, amp_sem, int_sem, out_sem = refs[11:]
    block, device_row, y, xh, k = where_am_i()
    col0 = block * COLS
    out0 = device_row * OUTS

    count_labels(inner, col0, COLS, in_n, 0)

    def int_copy(t):
        count = in_n[outer[out0 + t]]
        return count, pltpu.make_async_copy(
            ints.at[pl.ds(t * COLS, count)], int_buf.at[pl.ds(t * COLS, count)], int_sem.at[t]
        )

    int_copies = [int_copy(t) for t in range(OUTS)]
    for count, copy in int_copies:

        @pl.when(count > 0)
        def _(copy=copy):
            copy.start()

    def amp_copy(piece):
        at, offset, size, swapped, dy, dx, first = piece
        chip = ((y + dy) % 4) * 2 + (xh + dx) % 2
        start = (k ^ swapped) * cap + first if at else 0
        used = in_n[occ[2 * chip]] + in_n[occ[2 * chip + 1]]
        count = jnp.clip(used - start, 0, size)
        return count, pltpu.make_async_copy(
            lists[at].at[pl.ds(offset, count)],
            amp_buf.at[pl.ds(chip * 2 * cap + start, count)],
            amp_sem.at[amp_pieces.index(piece)],
        )

    amp_pieces = [(0, 0, 2 * cap, 0, 0, 0, 0)] + pieces(cap)
    amp_copies = [amp_copy(piece) for piece in amp_pieces]
    for count, copy in amp_copies:

        @pl.when(count > 0)
        def _(copy=copy):
            copy.start()

    for label in range(LABELS):
        row_n[label] = 0
        out_n[label] = 0

    def list_rows(r, carry):
        label = occ[r]
        row_at[label * ROWS + row_n[label]] = r
        row_n[label] += 1
        return carry

    lax.fori_loop(0, ROWS, list_rows, 0)

    def list_outs(t, carry):
        label = outer[out0 + t]
        out_at[label * OUTS + out_n[label]] = t
        out_n[label] += 1
        return carry

    lax.fori_loop(0, OUTS, list_outs, 0)

    for count, copy in int_copies + amp_copies:

        @pl.when(count > 0)
        def _(copy=copy):
            copy.wait()

    def out_copy(dest, slot):
        return pltpu.make_async_copy(
            out_buf.at[dest * 4 * OUTS + slot], part.at[dest, slot], out_sem.at[dest * 4 * OUTS + slot]
        )

    def per_label(label, carry):
        n_rows, n_outs, n_in = row_n[label], out_n[label], in_n[label]

        def left_of(starts, p, last):
            both = [
                jnp.concatenate(
                    [
                        amp_buf[at + p],
                        jnp.where(last == p, jnp.zeros((TILE, TILE), jnp.float32), amp_buf[at + last]),
                    ],
                    axis=1,
                )
                for at in starts
            ]
            hi, lo = split(jnp.concatenate(both, axis=0))
            return jnp.concatenate([lo, hi, hi], axis=1)

        def right_of(starts, p, last):
            def rows_of(part):
                return [jnp.concatenate([int_buf[at + w, part] for at in starts], axis=1) for w in (p, last)]

            return jnp.concatenate(rows_of(0) + rows_of(1) + rows_of(0), axis=0)

        def per_rows(rp, carry):
            ms = [jnp.minimum(ROW_BLOCK * rp + j, n_rows - 1) for j in range(ROW_BLOCK)]
            rs = [row_at[label * ROWS + m] for m in ms]
            starts = []
            for r in rs:
                chip = r // 2
                starts.append(chip * 2 * cap + jnp.where(r % 2 == 1, in_n[occ[2 * chip]], 0))

            def per_outs(up, carry):
                qs = [jnp.minimum(OUT_BLOCK * up + j, n_outs - 1) for j in range(OUT_BLOCK)]
                out_starts = [out_at[label * OUTS + q] * COLS for q in qs]

                def step(pp, total):
                    p = 2 * pp
                    last = jnp.minimum(p + 1, n_in - 1)
                    return total + jnp.dot(
                        left_of(starts, p, last),
                        right_of(out_starts, p, last),
                        preferred_element_type=jnp.float32,
                    )

                total = jnp.zeros((ROW_BLOCK * TILE, OUT_BLOCK * TILE), jnp.float32)
                total = lax.fori_loop(0, (n_in + 1) // 2, step, total)
                for rr, (m, r) in enumerate(zip(ms, rs)):
                    dest = (r // 2) % 4
                    before = jnp.where(r % 2 == 1, out_n[occ[r // 2 * 2]], 0)
                    low = out_n[occ[dest * 2]] + out_n[occ[dest * 2 + 1]]
                    before += jnp.where(r >= 8, low, 0)
                    for tt, q in enumerate(qs):
                        fresh = jnp.logical_and(m == ROW_BLOCK * rp + rr, q == OUT_BLOCK * up + tt)
                        value = total[rr * TILE : (rr + 1) * TILE, tt * TILE : (tt + 1) * TILE]

                        @pl.when(fresh)
                        def _(dest=dest, slot=before + q, value=value):
                            out_buf[dest * 4 * OUTS + slot] = value
                            out_copy(dest, slot).start()

                return carry

            return lax.fori_loop(0, (n_outs + OUT_BLOCK - 1) // OUT_BLOCK, per_outs, carry)

        return lax.fori_loop(0, (n_rows + ROW_BLOCK - 1) // ROW_BLOCK, per_rows, carry)

    lax.fori_loop(0, LABELS, per_label, 0)

    def drain_outs(dest, carry):
        def drain(slot, inner_carry):
            out_copy(dest, slot).wait()
            return inner_carry

        count = jnp.int32(0)
        for r in (0, 1, 8, 9):
            count += out_n[occ[dest * 2 + r]]
        return lax.fori_loop(0, count, drain, carry)

    lax.fori_loop(0, 4, drain_outs, 0)


def ladder(cap, occ, outer, inner, ints, lists):
    amps = ROWS * cap
    return pl.pallas_call(
        functools.partial(ladder_kernel, cap),
        out_shape=jax.ShapeDtypeStruct((4, 4 * OUTS, TILE, TILE), jnp.float32),
        in_specs=[SMEM] * 3 + [HBM] * (1 + len(lists)),
        out_specs=HBM,
        scratch_shapes=[
            pltpu.VMEM((amps, TILE, TILE), jnp.float32),
            pltpu.VMEM((OUTS * COLS, 2, TILE, TILE), jnp.bfloat16),
            pltpu.VMEM((OUTS * COLS, TILE, TILE), jnp.float32),
            pltpu.SMEM((LABELS,), jnp.int32),
            pltpu.SMEM((LABELS * ROWS,), jnp.int32),
            pltpu.SMEM((LABELS,), jnp.int32),
            pltpu.SMEM((LABELS * OUTS,), jnp.int32),
            pltpu.SMEM((LABELS,), jnp.int32),
            pltpu.SemaphoreType.DMA((23,)),
            pltpu.SemaphoreType.DMA((OUTS,)),
            pltpu.SemaphoreType.DMA((OUTS * COLS,)),
        ],
        compiler_params=pltpu.CompilerParams(vmem_limit_bytes=(18 + cap) * 1024 * 1024),
        name="ladder_tiles",
    )(occ, outer, inner, ints, *lists)


def gather_and_multiply(cap, packed, occ, outer, inner, ints):
    half = cap // 2
    core = lax.axis_index("ab") % 2
    send = functools.partial(lax.ppermute, axis_name="ab")
    own = lax.dynamic_slice_in_dim(packed, core * cap, cap)
    x_own = send(own, perm=X_SWAP)
    up = send(own, perm=Y_UP)
    down = send(own, perm=Y_DOWN)
    up_two = send(jnp.concatenate([x_own[:half], up[:half]]), perm=Y_UP)
    down_two = send(jnp.concatenate([x_own[half:], down[half:]]), perm=Y_DOWN)
    x_two = send(jnp.concatenate([up[half:], down[:half]]), perm=X_SWAP)
    ints = split_integrals(outer, inner, ints)
    up_two, down_two, ints = lax.optimization_barrier((up_two, down_two, ints))
    up_three = send(up_two[:half], perm=Y_UP)
    down_three = send(down_two[: cap - half], perm=Y_DOWN)
    lists = [packed, x_own, up, down, up_two, down_two, x_two, up_three, down_three]
    lists.append(send(jnp.concatenate([x_own, up, down, up_two, down_two, x_two]), perm=CORE_SWAP))
    lists.append(send(jnp.concatenate([up_three, down_three]), perm=CORE_SWAP))
    return ladder(cap, occ, outer, inner, ints, lists)


def place_kernel(cap_z, cap_w, occ, outer, first_rows, mine, other, out):
    block, device_row, _, _, _ = where_am_i()
    skip = jnp.maximum(first_rows[0] - (cap_z - cap_w), 0)
    slot = jnp.where(block >= 4, skip, 0)
    for r in range(2):
        label = occ[block * 2 + r]
        for t in range(OUTS):
            hit = outer[device_row * OUTS + t] == label
            at = jnp.minimum(slot, cap_w - 1)
            value = mine[at] + other[at]
            out[r * TILE : (r + 1) * TILE, t * TILE : (t + 1) * TILE] = jnp.where(
                hit, value, jnp.zeros_like(value)
            )
            slot = slot + hit.astype(jnp.int32)


def place(cap_z, cap_w, occ, outer, first_rows, mine, other):
    return pl.pallas_call(
        functools.partial(place_kernel, cap_z, cap_w),
        out_shape=jax.ShapeDtypeStruct((2 * TILE, OUTS * TILE), jnp.float32),
        in_specs=[SMEM] * 3 + [VMEM] * 2,
        out_specs=VMEM,
        compiler_params=pltpu.CompilerParams(vmem_limit_bytes=16 * 1024 * 1024),
        name="place_tiles",
    )(occ, outer, first_rows, mine, other)


def reduce_and_place(caps, part, occ, outer, first_rows):
    cap_z, cap_w = caps
    half = cap_z // 2
    c = lax.axis_index("cd")
    i = lax.axis_index("ij")
    send = functools.partial(lax.ppermute, axis_name="cd")

    def tiles(shift, first, size):
        return lax.dynamic_slice(part, ((c + shift) % 4, first, 0, 0), (1, size, TILE, TILE))[0]

    rest = cap_z - half
    up_far = send(tiles(2, 0, half), perm=Z_UP)
    down_far = send(tiles(2, half, rest), perm=Z_DOWN)
    from_down = send(jnp.concatenate([tiles(1, 0, half) + up_far, tiles(1, half, rest)]), perm=Z_UP)
    from_up = send(jnp.concatenate([tiles(3, 0, half), tiles(3, half, rest) + down_far]), perm=Z_DOWN)
    total = tiles(0, 0, cap_z) + from_down + from_up
    high = jnp.minimum(first_rows[0], cap_z - cap_w)
    mine = lax.dynamic_slice_in_dim(total, jnp.where(i == 1, high, 0), cap_w)
    theirs = lax.dynamic_slice_in_dim(total, jnp.where(i == 1, 0, high), cap_w)
    other = lax.ppermute(theirs, "ij", [(0, 1), (1, 0)])
    return place(cap_z, cap_w, occ, outer, first_rows, mine, other)


def shards(amplitudes, integrals, occupied_label, outer_label, inner_label):
    others = lax.ppermute(amplitudes, "ab", CORE_SWAP)
    amp_pick, out_pick, first_rows = plan(occupied_label, outer_label, inner_label)
    packed = pack(occupied_label, inner_label, amplitudes, others)
    part = lax.switch(
        amp_pick[0],
        [functools.partial(gather_and_multiply, cap) for cap in CAPS_T],
        packed, occupied_label, outer_label, inner_label, integrals,
    )
    return lax.switch(
        out_pick[0],
        [functools.partial(reduce_and_place, caps) for caps in CAPS_R],
        part, occupied_label, outer_label, first_rows,
    )


def solution(mesh):
    placed = (P("ab", ("ij", "cd")), P("ab", ("ij", "cd")), P(), P(), P())
    return jax.shard_map(
        shards, mesh=mesh, in_specs=placed, out_specs=P(("ij", "cd"), "ab"), check_vma=False
    )
```

```python
import functools

import jax
import jax.numpy as jnp
from jax import lax
from jax.experimental import pallas as pl
from jax.experimental.pallas import tpu as pltpu
from jax.sharding import PartitionSpec as P

TILE = 128
LABELS = 4
CAPS_T = (8, 12, 16)
CAPS_R = ((12, 8), (16, 8), (19, 12), (24, 14), (32, 16))
ROW_BLOCK = 4
OUT_BLOCK = 2
ROWS = 16
COLS = 16
OUTS = 8
SMEM = pl.BlockSpec(memory_space=pltpu.SMEM)
HBM = pl.BlockSpec(memory_space=pl.ANY)
VMEM = pl.BlockSpec(memory_space=pltpu.VMEM)


def ab_index(y, xh, k):
    return y * 4 + xh * 2 + k


PLACES = [(y, xh, k) for y in range(4) for xh in range(2) for k in range(2)]
CORE_SWAP = [(ab_index(y, x, k), ab_index(y, x, 1 - k)) for y, x, k in PLACES]
X_SWAP = [(ab_index(y, x, k), ab_index(y, 1 - x, k)) for y, x, k in PLACES]
Y_UP = [(ab_index(y, x, k), ab_index((y + 1) % 4, x, k)) for y, x, k in PLACES]
Y_DOWN = [(ab_index(y, x, k), ab_index((y + 3) % 4, x, k)) for y, x, k in PLACES]
Z_UP = [(c, (c + 1) % 4) for c in range(4)]
Z_DOWN = [(c, (c + 3) % 4) for c in range(4)]


def where_am_i():
    block = lax.axis_index("ij") * 4 + lax.axis_index("cd")
    device_row = lax.axis_index("ab")
    return block, device_row, device_row // 4, (device_row // 2) % 2, device_row % 2


def count_labels(labels, first, size, counts, base):
    for label in range(LABELS):
        counts[base + label] = 0

    def add(at, carry):
        counts[base + labels[first + at]] += 1
        return carry

    lax.fori_loop(0, size, add, 0)


def plan_kernel(occ, outer, inner, amp_pick, out_pick, first_rows):
    def counts_of(labels, first, size):
        counts = jnp.int32(0)
        for at in range(size):
            counts += lax.shift_left(jnp.int32(1), labels[first + at] * 8)
        return counts

    row_shift = [occ[r] * 8 for r in range(ROWS)]

    def rows_of(counts, r):
        return sum(lax.shift_right_logical(counts, row_shift[r + half]) & 255 for half in range(2))

    def amp_block(block, need):
        counts = counts_of(inner, block * COLS, COLS)
        for chip in range(ROWS // 2):
            need = jnp.maximum(need, rows_of(counts, 2 * chip))
        return need

    need = lax.fori_loop(0, 8, amp_block, jnp.int32(0))
    pick = jnp.int32(0)
    for cap in CAPS_T[:-1]:
        pick += (need > 2 * cap).astype(jnp.int32)
    amp_pick[0] = pick

    def out_block(block, needs):
        need_w, need_z = needs
        counts = counts_of(outer, block * OUTS, OUTS)
        for c in range(4):
            low, high = rows_of(counts, 2 * c), rows_of(counts, 2 * c + 8)
            need_w = jnp.maximum(need_w, jnp.maximum(low, high))
            need_z = jnp.maximum(need_z, low + high)
        return need_w, need_z

    need_w, need_z = lax.fori_loop(0, ROWS, out_block, (jnp.int32(0), jnp.int32(0)))
    pick = jnp.int32(0)
    for cap_z, cap_w in CAPS_R[:-1]:
        pick += jnp.logical_or(need_w > cap_w, need_z > cap_z).astype(jnp.int32)
    out_pick[0] = pick
    counts = counts_of(outer, lax.axis_index("ab") * OUTS, OUTS)
    c = lax.axis_index("cd")
    first_rows[0] = sum(
        lax.shift_right_logical(counts, occ[2 * c + half] * 8) & 255 for half in range(2)
    )


def plan(occ, outer, inner):
    one = jax.ShapeDtypeStruct((1,), jnp.int32)
    return pl.pallas_call(
        plan_kernel,
        out_shape=(one, one, one),
        in_specs=[SMEM] * 3,
        out_specs=(SMEM, SMEM, SMEM),
        name="plan_capacities",
    )(occ, outer, inner)


def pack_kernel(occ, inner, mine, other, packed, sem):
    block, _, y, xh, k = where_am_i()
    chip = y * 2 + xh

    def tile(ref, c):
        return ref.at[:, pl.ds(pl.multiple_of(c * TILE, TILE), TILE)]

    def issue(core, first):
        label = occ[chip * 2 + core]

        def one(c, p):
            hit = inner[block * COLS + c] == label

            @pl.when(jnp.logical_and(hit, core == k))
            def _():
                pltpu.make_async_copy(tile(mine, c), packed.at[p], sem.at[p]).start()

            @pl.when(jnp.logical_and(hit, core != k))
            def _():
                pltpu.make_async_copy(tile(other, c), packed.at[p], sem.at[p]).start()

            return p + hit.astype(jnp.int32)

        return lax.fori_loop(0, COLS, one, first)

    count = issue(1, issue(0, jnp.int32(0)))

    def drain(p, carry):
        pltpu.make_async_copy(tile(mine, 0), packed.at[p], sem.at[p]).wait()
        return carry

    lax.fori_loop(0, count, drain, 0)


def pack(occ, inner, mine, other):
    return pl.pallas_call(
        pack_kernel,
        out_shape=jax.ShapeDtypeStruct((2 * COLS, TILE, TILE), jnp.float32),
        in_specs=[SMEM, SMEM, HBM, HBM],
        out_specs=HBM,
        scratch_shapes=[pltpu.SemaphoreType.DMA((2 * COLS,))],
        name="pack_amplitudes",
    )(occ, inner, mine, other)


def split(x):
    hi = x.astype(jnp.bfloat16)
    lo = (x - hi.astype(jnp.float32)).astype(jnp.bfloat16)
    return hi, lo


def split_kernel(outer, inner, ints, parts, buf, sem):
    block, device_row, _, _, _ = where_am_i()
    col0 = block * COLS
    out0 = device_row * OUTS

    def copy(t, c, p):
        return pltpu.make_async_copy(
            ints.at[pl.ds(pl.multiple_of(t * TILE, TILE), TILE), pl.ds(pl.multiple_of(c * TILE, TILE), TILE)],
            buf.at[t * COLS + p],
            sem.at[t * COLS + p],
        )

    def count(t, use):
        label = outer[out0 + t]

        def one(c, p):
            hit = inner[col0 + c] == label
            if use:

                @pl.when(hit)
                def _():
                    copy(t, c, p).start()

            return p + hit.astype(jnp.int32)

        return lax.fori_loop(0, COLS, one, jnp.int32(0))

    def issue(t, carry):
        count(t, True)
        return carry

    lax.fori_loop(0, OUTS, issue, 0)

    def split_all(t, carry):
        def one(p, inner_carry):
            copy(t, 0, p).wait()
            at = t * COLS + p
            parts[at, 0], parts[at, 1] = split(buf[at].T)
            return inner_carry

        return lax.fori_loop(0, count(t, False), one, carry)

    lax.fori_loop(0, OUTS, split_all, 0)


def split_integrals(outer, inner, ints):
    return pl.pallas_call(
        split_kernel,
        out_shape=jax.ShapeDtypeStruct((OUTS * COLS, 2, TILE, TILE), jnp.bfloat16),
        in_specs=[SMEM, SMEM, HBM],
        out_specs=VMEM,
        scratch_shapes=[
            pltpu.VMEM((OUTS * COLS, TILE, TILE), jnp.float32),
            pltpu.SemaphoreType.DMA((OUTS * COLS,)),
        ],
        compiler_params=pltpu.CompilerParams(vmem_limit_bytes=20 * 1024 * 1024),
        cost_estimate=pl.CostEstimate(flops=0, bytes_accessed=1024, transcendentals=0),
        name="split_integrals",
    )(outer, inner, ints)


def pieces(cap):
    half = cap // 2
    rest = cap - half
    early = [
        (0, cap, 0, 1, 0),
        (cap, cap, 3, 0, 0),
        (2 * cap, cap, 1, 0, 0),
        (3 * cap, half, 3, 1, 0),
        (3 * cap + half, half, 2, 0, 0),
        (3 * cap + 2 * half, rest, 1, 1, half),
        (3 * cap + 2 * half + rest, rest, 2, 0, half),
        (5 * cap, rest, 3, 1, half),
        (5 * cap + rest, half, 1, 1, 0),
    ]
    late = [(0, half, 2, 1, 0), (half, rest, 2, 1, half)]
    return early, late


def ladder_kernel(cap, occ, outer, inner, ints, *refs):
    packed, early, early_other, late, late_other = refs[:5]
    part, amp_buf, int_buf, out_buf, row_n, row_at, out_n, out_at, in_n, table, fill_sem, out_sem = refs[5:]
    block, device_row, y, xh, k = where_am_i()
    col0 = block * COLS
    out0 = device_row * OUTS

    count_labels(inner, col0, COLS, in_n, 0)

    def fill_ints(t, total):
        count = in_n[outer[out0 + t]]

        @pl.when(count > 0)
        def _():
            pltpu.make_async_copy(
                ints.at[pl.ds(t * COLS, count)], int_buf.at[pl.ds(t * COLS, count)], fill_sem.at[0]
            ).start()

        return total + count

    int_total = lax.fori_loop(0, OUTS, fill_ints, jnp.int32(0))

    def fill_amps(src, offset, size, chip, start):
        used = in_n[occ[2 * chip]] + in_n[occ[2 * chip + 1]]
        count = jnp.clip(used - start, 0, size)

        @pl.when(count > 0)
        def _():
            pltpu.make_async_copy(
                src.at[pl.ds(offset, count)],
                amp_buf.at[pl.ds(chip * 2 * cap + start, count)],
                fill_sem.at[1],
            ).start()

    fill_amps(packed, 0, 2 * cap, y * 2 + xh, 0)
    early_pieces, late_pieces = pieces(cap)
    fields = len(early_pieces[0])
    for at, piece in enumerate(early_pieces + late_pieces):
        for field, value in enumerate(piece):
            table[at * fields + field] = value

    def fill_piece(sources):
        def one(at, carry):
            offset, size, dy, dx, first = (table[at * fields + field] for field in range(fields))
            chip = ((y + dy) % 4) * 2 + (xh + dx) % 2
            for swapped, src in enumerate(sources):
                fill_amps(src, offset, size, chip, (k ^ swapped) * cap + first)
            return carry

        return one

    n_early = len(early_pieces)
    lax.fori_loop(0, n_early, fill_piece((early, early_other)), 0)
    lax.fori_loop(n_early, n_early + len(late_pieces), fill_piece((late, late_other)), 0)

    for label in range(LABELS):
        row_n[label] = 0
        out_n[label] = 0

    def list_rows(r, carry):
        label = occ[r]
        row_at[label * ROWS + row_n[label]] = r
        row_n[label] += 1
        return carry

    lax.fori_loop(0, ROWS, list_rows, 0)

    def list_outs(t, carry):
        label = outer[out0 + t]
        out_at[label * OUTS + out_n[label]] = t
        out_n[label] += 1
        return carry

    lax.fori_loop(0, OUTS, list_outs, 0)

    amp_total = jnp.int32(0)
    for r in range(ROWS):
        amp_total += in_n[occ[r]]
    for at, (total, buf) in enumerate(((int_total, int_buf), (amp_total, amp_buf))):

        @pl.when(total > 0)
        def _(at=at, total=total, buf=buf):
            filled = buf.at[pl.ds(0, total)]
            pltpu.make_async_copy(filled, filled, fill_sem.at[at]).wait()

    def out_copy(dest, slot):
        return pltpu.make_async_copy(
            out_buf.at[dest * 4 * OUTS + slot], part.at[dest, slot], out_sem.at[dest * 4 * OUTS + slot]
        )

    def per_label(label, carry):
        n_rows, n_outs, n_in = row_n[label], out_n[label], in_n[label]

        def left_of(starts, p, last):
            both = [
                jnp.concatenate(
                    [
                        amp_buf[at + p],
                        jnp.where(last == p, jnp.zeros((TILE, TILE), jnp.float32), amp_buf[at + last]),
                    ],
                    axis=1,
                )
                for at in starts
            ]
            hi, lo = split(jnp.concatenate(both, axis=0))
            return jnp.concatenate([lo, hi, hi], axis=1)

        def right_of(starts, p, last):
            def rows_of(part):
                return [jnp.concatenate([int_buf[at + w, part] for at in starts], axis=1) for w in (p, last)]

            return jnp.concatenate(rows_of(0) + rows_of(1) + rows_of(0), axis=0)

        def per_rows(rp, carry):
            ms = [jnp.minimum(ROW_BLOCK * rp + j, n_rows - 1) for j in range(ROW_BLOCK)]
            rs = [row_at[label * ROWS + m] for m in ms]
            starts = []
            for r in rs:
                chip = r // 2
                starts.append(chip * 2 * cap + jnp.where(r % 2 == 1, in_n[occ[2 * chip]], 0))

            def per_outs(up, carry):
                qs = [jnp.minimum(OUT_BLOCK * up + j, n_outs - 1) for j in range(OUT_BLOCK)]
                out_starts = [out_at[label * OUTS + q] * COLS for q in qs]

                def step(pp, total):
                    p = 2 * pp
                    last = jnp.minimum(p + 1, n_in - 1)
                    return total + jnp.dot(
                        left_of(starts, p, last),
                        right_of(out_starts, p, last),
                        preferred_element_type=jnp.float32,
                    )

                total = jnp.zeros((ROW_BLOCK * TILE, OUT_BLOCK * TILE), jnp.float32)
                total = lax.fori_loop(0, (n_in + 1) // 2, step, total)
                for rr, (m, r) in enumerate(zip(ms, rs)):
                    dest = (r // 2) % 4
                    before = jnp.where(r % 2 == 1, out_n[occ[r // 2 * 2]], 0)
                    low = out_n[occ[dest * 2]] + out_n[occ[dest * 2 + 1]]
                    before += jnp.where(r >= 8, low, 0)
                    for tt, q in enumerate(qs):
                        fresh = jnp.logical_and(m == ROW_BLOCK * rp + rr, q == OUT_BLOCK * up + tt)
                        value = total[rr * TILE : (rr + 1) * TILE, tt * TILE : (tt + 1) * TILE]

                        @pl.when(fresh)
                        def _(dest=dest, slot=before + q, value=value):
                            out_buf[dest * 4 * OUTS + slot] = value
                            out_copy(dest, slot).start()

                return carry

            return lax.fori_loop(0, (n_outs + OUT_BLOCK - 1) // OUT_BLOCK, per_outs, carry)

        return lax.fori_loop(0, (n_rows + ROW_BLOCK - 1) // ROW_BLOCK, per_rows, carry)

    lax.fori_loop(0, LABELS, per_label, 0)

    def drain_outs(dest, carry):
        def drain(slot, inner_carry):
            out_copy(dest, slot).wait()
            return inner_carry

        count = jnp.int32(0)
        for r in (0, 1, 8, 9):
            count += out_n[occ[dest * 2 + r]]
        return lax.fori_loop(0, count, drain, carry)

    lax.fori_loop(0, 4, drain_outs, 0)


def ladder(cap, occ, outer, inner, ints, lists):
    amps = ROWS * cap
    return pl.pallas_call(
        functools.partial(ladder_kernel, cap),
        out_shape=jax.ShapeDtypeStruct((4, 4 * OUTS, TILE, TILE), jnp.float32),
        in_specs=[SMEM] * 3 + [HBM] * (1 + len(lists)),
        out_specs=pl.BlockSpec(memory_space=pltpu.HBM),
        scratch_shapes=[
            pltpu.VMEM((amps, TILE, TILE), jnp.float32),
            pltpu.VMEM((OUTS * COLS, 2, TILE, TILE), jnp.bfloat16),
            pltpu.VMEM((OUTS * COLS, TILE, TILE), jnp.float32),
            pltpu.SMEM((LABELS,), jnp.int32),
            pltpu.SMEM((LABELS * ROWS,), jnp.int32),
            pltpu.SMEM((LABELS,), jnp.int32),
            pltpu.SMEM((LABELS * OUTS,), jnp.int32),
            pltpu.SMEM((LABELS,), jnp.int32),
            pltpu.SMEM((64,), jnp.int32),
            pltpu.SemaphoreType.DMA((2,)),
            pltpu.SemaphoreType.DMA((OUTS * COLS,)),
        ],
        compiler_params=pltpu.CompilerParams(vmem_limit_bytes=(18 + cap) * 1024 * 1024),
        name="ladder_tiles",
    )(occ, outer, inner, ints, *lists)


def gather_and_multiply(cap, packed, occ, outer, inner, ints):
    half = cap // 2
    core = lax.axis_index("ab") % 2
    send = functools.partial(lax.ppermute, axis_name="ab")
    own = lax.dynamic_slice_in_dim(packed, core * cap, cap)
    x_own = send(own, perm=X_SWAP)
    up = send(own, perm=Y_UP)
    down = send(own, perm=Y_DOWN)
    rest = cap - half
    to_up = jnp.concatenate([x_own[:half], up[:half]])
    to_down = jnp.concatenate([x_own[half:], down[half:]])
    to_x = jnp.concatenate([up[half:], down[:half]])
    to_up, to_down, to_x, ints = lax.optimization_barrier((to_up, to_down, to_x, ints))
    x_two = send(to_x, perm=X_SWAP)
    up_two = send(to_up, perm=Y_UP)
    down_two = send(to_down, perm=Y_DOWN)
    ints = split_integrals(outer, inner, ints)
    up_two, down_two, ints = lax.optimization_barrier((up_two, down_two, ints))
    up_three = send(up_two[:half], perm=Y_UP)
    down_three = send(down_two[:rest], perm=Y_DOWN)
    early = jnp.concatenate([x_own, up, down, up_two, down_two, x_two])
    early_other = send(early, perm=CORE_SWAP)
    late = jnp.concatenate([up_three, down_three])
    late_other = send(late, perm=CORE_SWAP)
    return ladder(cap, occ, outer, inner, ints, [packed, early, early_other, late, late_other])


def place_kernel(cap_z, cap_w, occ, outer, first_rows, mine, other, out):
    block, device_row, _, _, _ = where_am_i()
    skip = jnp.maximum(first_rows[0] - (cap_z - cap_w), 0)
    slot = jnp.where(block >= 4, skip, 0)
    for r in range(2):
        label = occ[block * 2 + r]
        for t in range(OUTS):
            hit = outer[device_row * OUTS + t] == label
            at = jnp.minimum(slot, cap_w - 1)
            value = mine[at] + other[at]
            out[r * TILE : (r + 1) * TILE, t * TILE : (t + 1) * TILE] = jnp.where(
                hit, value, jnp.zeros_like(value)
            )
            slot = slot + hit.astype(jnp.int32)


def place(cap_z, cap_w, occ, outer, first_rows, mine, other):
    return pl.pallas_call(
        functools.partial(place_kernel, cap_z, cap_w),
        out_shape=jax.ShapeDtypeStruct((2 * TILE, OUTS * TILE), jnp.float32),
        in_specs=[SMEM] * 3 + [VMEM] * 2,
        out_specs=VMEM,
        compiler_params=pltpu.CompilerParams(vmem_limit_bytes=16 * 1024 * 1024),
        name="place_tiles",
    )(occ, outer, first_rows, mine, other)


def reduce_and_place(caps, part, occ, outer, first_rows):
    cap_z, cap_w = caps
    half = cap_z // 2
    c = lax.axis_index("cd")
    i = lax.axis_index("ij")
    send = functools.partial(lax.ppermute, axis_name="cd")

    def tiles(shift, first, size):
        return lax.dynamic_slice(part, ((c + shift) % 4, first, 0, 0), (1, size, TILE, TILE))[0]

    rest = cap_z - half
    up_far = send(tiles(2, 0, half), perm=Z_UP)
    down_far = send(tiles(2, half, rest), perm=Z_DOWN)
    from_down = send(jnp.concatenate([tiles(1, 0, half) + up_far, tiles(1, half, rest)]), perm=Z_UP)
    from_up = send(jnp.concatenate([tiles(3, 0, half), tiles(3, half, rest) + down_far]), perm=Z_DOWN)
    total = tiles(0, 0, cap_z) + from_down + from_up
    high = jnp.minimum(first_rows[0], cap_z - cap_w)
    mine = lax.dynamic_slice_in_dim(total, jnp.where(i == 1, high, 0), cap_w)
    theirs = lax.dynamic_slice_in_dim(total, jnp.where(i == 1, 0, high), cap_w)
    other = lax.ppermute(theirs, "ij", [(0, 1), (1, 0)])
    return place(cap_z, cap_w, occ, outer, first_rows, mine, other)


def shards(amplitudes, integrals, occupied_label, outer_label, inner_label):
    others = lax.ppermute(amplitudes, "ab", CORE_SWAP)
    amp_pick, out_pick, first_rows = plan(occupied_label, outer_label, inner_label)
    packed = pack(occupied_label, inner_label, amplitudes, others)
    part = lax.switch(
        amp_pick[0],
        [functools.partial(gather_and_multiply, cap) for cap in CAPS_T],
        packed, occupied_label, outer_label, inner_label, integrals,
    )
    return lax.switch(
        out_pick[0],
        [functools.partial(reduce_and_place, caps) for caps in CAPS_R],
        part, occupied_label, outer_label, first_rows,
    )


def solution(mesh):
    placed = (P("ab", ("ij", "cd")), P("ab", ("ij", "cd")), P(), P(), P())
    return jax.shard_map(
        shards, mesh=mesh, in_specs=placed, out_specs=P(("ij", "cd"), "ab"), check_vma=False
    )
```
